128 devices in a mesh: pb: 64 (over z, x, y_lo, core), row: 2 (over y_hi).
Axes of the slice: x: 4, y: 4 (y_hi: 2, y_lo: 2; y = y_hi * 2 + y_lo), z: 4, core: 2. Of those that a mesh axis runs over, the one named last changes fastest.
Arguments:
- queries: bfloat16 [16384, 512], P('pb'), may hold values from -6 to 6
- references: bfloat16 [2, 4096, 512], P('row', 'pb'), may hold values from -6 to 6
- ratios: int32 [4, 2], replicated, may hold values from 1 to 3, as said below
- lengths: int32 [4], replicated, may hold values from 2 to 24, as said below
Outputs:
- enhanced: bfloat16 [16384, 8192], P('pb', 'row')
The draws below stay inside these ranges and needn't reach their ends.
Inputs may be any that keep to these rules, and one draw needn't show every extreme that they name: `ratios`: the two steps of a direction differ, and no two directions have the same pair of steps. `lengths`: at least one direction has exactly 24 taps.
All inputs are finite; a program needn't handle non-finite values.
Results may differ from the reference program's by a relative error of at most 0.001.
Values may be sent and summed in bfloat16 or wider, within the bound.
A program may use at most 64 MiB of HBM per device.

```python
import math
import jax
import jax.numpy as jnp
from jax import lax

E = 512
NDIR = 4
LMAX = 24
HALVES = 2
REF_HALF = 4096
NQ = 16384
NR = 8192


def draw_ratios(key, part):
    key = jax.random.fold_in(key, 29)
    codes = jax.random.permutation(key, jnp.arange(6, dtype=jnp.int32))[:NDIR]
    group = codes // 2
    smaller = 1 + group // 2
    bigger = 2 + jnp.minimum(group, 1)
    flip = codes % 2
    first = jnp.where(flip == 1, bigger, smaller)
    second = jnp.where(flip == 1, smaller, bigger)
    return jnp.stack([first, second], axis=1).astype(jnp.int32)


def draw_lengths(key, part):
    key_values, key_choice = jax.random.split(jax.random.fold_in(key, 17))
    values = jax.random.randint(key_values, (NDIR,), 2, LMAX + 1, dtype=jnp.int32)
    chosen = jax.random.randint(key_choice, (), 0, NDIR, dtype=jnp.int32)
    return jnp.where(jnp.arange(NDIR, dtype=jnp.int32) == chosen, LMAX, values).astype(jnp.int32)


def shard_levels(own_key, shape, cuts, smallest, largest):
    factor_of, own = 1.0, jax.random.fold_in(own_key, 6)
    for dim, shards_of in cuts:
        draws = jnp.exp(jax.random.uniform(jax.random.fold_in(own, dim), (shards_of,), jnp.float32, smallest / len(cuts), largest / len(cuts)))
        factor_of = factor_of * jnp.repeat(draws, shape[dim] // shards_of).reshape([-1 if axis == dim else 1 for axis in range(len(shape))])
    return factor_of


def normal_values(own_key, dims, scale, reach, cuts=(), held_as=jnp.bfloat16):
    factor_of = shard_levels(own_key, dims, cuts, -0.22, 0.18) if cuts else 1.0
    array = jax.random.normal(own_key, dims, jnp.float32) * scale * factor_of
    return jnp.minimum(jnp.maximum(array, -reach), reach).astype(held_as)


def setup_inputs(seed: int = 0) -> dict:
    key_list = jax.random.split(jax.random.key(seed), 5)
    queries = normal_values(key_list[0], (NQ, E), 1.0, 6.0, ((0, 64),))
    references = normal_values(key_list[1], (HALVES, REF_HALF, E), 1.0, 6.0, ((0, 2), (1, 64)))
    ratios = draw_ratios(jax.random.fold_in(key_list[4], 71), 0)
    lengths = draw_lengths(jax.random.fold_in(key_list[4], 71), 0)
    return {"queries": queries, "references": references, "ratios": ratios, "lengths": lengths}


def offsets(ratios, lengths):
    tap_range = jnp.arange(LMAX, dtype=jnp.int32)
    steps_query = ratios[:, 0]
    steps_ref = ratios[:, 1]
    larger = jnp.maximum(steps_query, steps_ref)
    along_query = tap_range[None, :] * steps_query[:, None] // larger[:, None]
    along_ref = tap_range[None, :] * steps_ref[:, None] // larger[:, None]
    inverse = 1.0 / lengths.astype(jnp.float32)
    tap_weights = jnp.where(tap_range[None, :] < lengths[:, None], inverse[:, None], 0.0).astype(jnp.float32)
    return (along_query, along_ref, tap_weights)

def smooth(similarity, along_query, along_ref, tap_weights, row_count, col_count):
    strongest = None
    for direction in range(NDIR):
        running = jnp.zeros((row_count, col_count), jnp.float32)
        for tap_index in range(LMAX):
            shifted = lax.dynamic_slice(similarity, (along_query[direction, tap_index], along_ref[direction, tap_index]), (row_count, col_count))
            running = running + tap_weights[direction, tap_index] * shifted
        strongest = running if strongest is None else jnp.maximum(strongest, running)
    return strongest

def reference(queries, references, ratios, lengths):
    along_query, along_ref, tap_weights = offsets(ratios, lengths)
    margin = LMAX - 1
    inv_root = 1.0 / math.sqrt(E)
    flat = references.reshape(NR, E)
    padded_ref = jnp.concatenate([flat, jnp.zeros((margin, E), jnp.bfloat16)], axis=0)
    padded_queries = jnp.concatenate([queries, jnp.zeros((margin, E), jnp.bfloat16)], axis=0)
    block_rows = min(512, NQ)

    def one_block(block_index):
        slab = lax.dynamic_slice_in_dim(padded_queries, block_index * block_rows, block_rows + margin, 0)
        similarity = jnp.dot(slab, padded_ref.T, preferred_element_type=jnp.float32) * inv_root
        return smooth(similarity, along_query, along_ref, tap_weights, block_rows, NR).astype(jnp.bfloat16)
    result = lax.map(one_block, jnp.arange(NQ // block_rows, dtype=jnp.int32))
    return result.reshape(NQ, NR)
```

```python
import functools
import math

import jax
import jax.numpy as jnp
from jax import lax
from jax.experimental import pallas as pl
from jax.experimental.pallas import tpu as pltpu
from jax.sharding import PartitionSpec as P

E = 512
MESH = pl.DeviceIdType.MESH
TAIL = 32


def gather(q_ref, r_ref, g, qh, rh, local, ysem, u1, u2, v1, v2, sib, hsem):
    pb, row = lax.axis_index("pb"), lax.axis_index("row")
    pbs = 64
    c, y, x, z = pb & 1, (pb >> 1) & 1, (pb >> 2) & 3, pb >> 4

    def at(z_, x_, y_, c_):
        return ((z_ * 4 + x_) * 2 + y_) * 2 + c_

    me = (z, x)
    def place(axis, k):
        return (z, (x + k) & 3) if axis == 0 else ((z + k) & 3, x)

    left = [at(*place(a, 3), y, c) for a in range(2)]
    right = [at(*place(a, 1), y, c) for a in range(2)]
    other_y = at(z, x, 1 - y, c)
    other_c = at(z, x, y, 1 - c)

    bar = pltpu.get_barrier_semaphore()
    for dev in (left[0], right[0], left[1], right[1], other_y, other_c):
        pl.semaphore_signal(bar, inc=1, device_id={"pb": dev}, device_id_type=MESH)

    @pl.when(pb < pbs - 1)
    def _():
        pl.semaphore_signal(bar, inc=1, device_id={"pb": pb + 1}, device_id_type=MESH)

    @pl.when(row == 0)
    def _():
        pl.semaphore_signal(bar, inc=1, device_id={"row": 1}, device_id_type=MESH)
    pl.semaphore_wait(bar, 6 + jnp.minimum(pb, 1) + row)

    sends = []

    def send(src, dst, sems, k, dev):
        copy = pltpu.make_async_remote_copy(src_ref=src, dst_ref=dst, send_sem=sems.at[0, k], recv_sem=sems.at[1, k],
                                            device_id={"pb": dev}, device_id_type=MESH)
        copy.start()
        sends.append(copy)

    def arrived(dst, sems, k):
        pltpu.make_async_copy(dst, dst, sems.at[1, k]).wait()

    def block(zx, y_, c_, lo, size):
        return g.at[zx[0], zx[1], y_, c_, pl.ds(lo, size)]

    def pair(zx, c_, lo, size):
        return g.at[zx[0], zx[1], :, c_, pl.ds(lo, size)]

    own_block = block(me, y, c, 0, 64)
    keep = pltpu.make_async_copy(r_ref.at[0], own_block, local)
    keep.start()
    send(r_ref.at[0], own_block, ysem, 0, other_y)
    for h in range(2):
        mine = r_ref.at[0, pl.ds(32 * h, 32)]
        send(mine, block(me, y, c, 32 * h, 32), u1, h * 4 + 0, right[h])
        send(mine, block(me, y, c, 32 * h, 32), u1, h * 4 + 1, left[h])
    send(r_ref.at[0], own_block, sib, 0, other_c)
    first = pltpu.make_async_remote_copy(src_ref=q_ref.at[pl.ds(0, TAIL)], dst_ref=qh, send_sem=hsem.at[0, 0], recv_sem=hsem.at[1, 0],
                                         device_id={"pb": jnp.maximum(pb - 1, 0)}, device_id_type=MESH)

    @pl.when(pb > 0)
    def _():
        first.start()

    keep.wait()
    arrived(block(me, 1 - y, c, 0, 64), ysem, 0)
    for h in range(2):
        theirs = block(me, 1 - y, c, 32 * h, 32)
        send(theirs, theirs, u1, h * 4 + 2, right[h])
        send(theirs, theirs, u1, h * 4 + 3, left[h])
    far = [1, 0]
    for h in range(2):
        p = pair(me, c, 32 * h, 32)
        send(p, p, v1, h * 8 + 0, right[far[h]])
        send(p, p, v1, h * 8 + 1, left[far[h]])
    theirs = block(me, 1 - y, c, 0, 64)
    send(theirs, theirs, sib, 1, other_c)
    n = 2
    for h in range(2):
        for side, k in ((0, 3), (1, 1)):
            src = place(h, k)
            for w, y_ in ((0, y), (1, 1 - y)):
                arrived(block(src, y_, c, 32 * h, 32), u1, h * 4 + 2 * w + side)
                piece = block(src, y_, c, 32 * h + 16 * side, 16)
                send(piece, piece, u2, h * 4 + 2 * w + side, right[h] if side == 0 else left[h])
    for h in range(2):
        for side, k in ((0, 3), (1, 1)):
            p = pair(place(h, k), c, 32 * h, 32)
            send(p, p, v1, h * 8 + 2 + 2 * side, right[far[h]])
            send(p, p, v1, h * 8 + 3 + 2 * side, left[far[h]])
            send(p, p, sib, n, other_c)
            n += 1
    for h in range(2):
        src = place(h, 2)
        for side in range(2):
            for w, y_ in ((0, y), (1, 1 - y)):
                arrived(block(src, y_, c, 32 * h + 16 * side, 16), u2, h * 4 + 2 * w + side)
        p = pair(src, c, 32 * h, 32)
        send(p, p, v1, h * 8 + 6, right[far[h]])
        send(p, p, v1, h * 8 + 7, left[far[h]])
        send(p, p, sib, n, other_c)
        n += 1

    def spot(h, k1, k2):
        return ((z + k2) & 3, (x + k1) & 3) if h == 0 else ((z + k1) & 3, (x + k2) & 3)

    steps = (0, 3, 1, 2)
    for j, k1 in enumerate(steps):
        for h in range(2):
            for side, k2 in ((0, 3), (1, 1)):
                src = spot(h, k1, k2)
                p = pair(src, c, 32 * h, 32)
                arrived(p, v1, h * 8 + 2 * j + side)
                piece = pair(src, c, 32 * h + 16 * side, 16)
                send(piece, piece, v2, h * 8 + 2 * j + side, right[far[h]] if side == 0 else left[far[h]])
                send(p, p, sib, n, other_c)
                n += 1
    for j, k1 in enumerate(steps):
        for h in range(2):
            src = spot(h, k1, 2)
            for side in range(2):
                arrived(pair(src, c, 32 * h + 16 * side, 16), v2, h * 8 + 2 * j + side)
            p = pair(src, c, 32 * h, 32)
            send(p, p, sib, n, other_c)
            n += 1
    o = 1 - c
    arrived(block(me, y, o, 0, 64), sib, 0)
    arrived(block(me, 1 - y, o, 0, 64), sib, 1)
    n = 2
    for h in range(2):
        for k in (3, 1):
            arrived(pair(place(h, k), o, 32 * h, 32), sib, n)
            n += 1
    for h in range(2):
        arrived(pair(place(h, 2), o, 32 * h, 32), sib, n)
        n += 1
    for k1 in steps:
        for h in range(2):
            for k2 in (3, 1):
                arrived(pair(spot(h, k1, k2), o, 32 * h, 32), sib, n)
                n += 1
    for k1 in steps:
        for h in range(2):
            arrived(pair(spot(h, k1, 2), o, 32 * h, 32), sib, n)
            n += 1
    head = pltpu.make_async_remote_copy(src_ref=g.at[0, 0, 0, 0, pl.ds(0, TAIL)], dst_ref=rh, send_sem=hsem.at[0, 1], recv_sem=hsem.at[1, 1],
                                        device_id={"row": 0}, device_id_type=MESH)

    @pl.when(row == 1)
    def _():
        head.start()

    for copy in sends:
        copy.wait_send()

    @pl.when(pb > 0)
    def _():
        first.wait_send()

    @pl.when(pb < pbs - 1)
    def _():
        first.wait_recv()

    @pl.when(row == 1)
    def _():
        head.wait_send()

    @pl.when(row == 0)
    def _():
        head.wait_recv()


def call_gather(q, r):
    bf = jnp.bfloat16
    D = pltpu.SemaphoreType.DMA
    g, qh, rh = pl.pallas_call(
        gather,
        out_shape=(jax.ShapeDtypeStruct((4, 4, 2, 2, 64, E), bf), jax.ShapeDtypeStruct((TAIL, E), bf), jax.ShapeDtypeStruct((TAIL, E), bf)),
        in_specs=[pl.BlockSpec(memory_space=pl.ANY)] * 2,
        out_specs=[pl.BlockSpec(memory_space=pl.ANY)] * 3,
        scratch_shapes=[D, D((2, 1)), D((2, 8)), D((2, 8)), D((2, 16)), D((2, 16)), D((2, 32)), D((2, 2))],
        compiler_params=pltpu.CompilerParams(collective_id=0, has_side_effects=True),
        name="gather",
    )(q, r)
    return g.reshape(4096, E), qh, rh


NDIR = 4
LMAX = 24
B = 32
HALO = 24
PLANES = B + HALO
ZERO = 58
ROWS = 288
PAD = 296
SUPER = 32


def lane_iota(shape, d):
    return lax.broadcasted_iota(jnp.int32, shape, d)


def compute(ratios, lengths, q_ref, qh_ref, rh_ref, g_ref, out_ref,
            gv, qx, rb, s, d0, d1, d2, d3, e0, e1, e2, e3, o, perm, osb, gsem, osem):
    rows = q_ref.shape[0]
    cols = g_ref.shape[0]
    parts = 4
    part = cols // parts
    ds, es = (d0, d1, d2, d3), (e0, e1, e2, e3)
    copies = [pltpu.make_async_copy(g_ref.at[pl.ds(k * part, part)], gv.at[pl.ds(k * part, part)], gsem.at[k]) for k in range(parts)]
    for c in copies:
        c.start()
    qx[pl.ds(0, rows), :] = q_ref[...]
    keep_q = lax.axis_index("pb") < lax.axis_size("pb") - 1
    keep_r = lax.axis_index("row") == 0
    qx[pl.ds(rows, 32), :] = jnp.where(keep_q, qh_ref[...], jnp.zeros((32, E), jnp.bfloat16))
    rhv = jnp.where(keep_r, rh_ref[...], jnp.zeros((32, E), jnp.bfloat16))
    ps = [ratios[d, 0] for d in range(NDIR)]
    ss = [ratios[d, 1] for d in range(NDIR)]
    ms = [jnp.maximum(ps[d], ss[d]) for d in range(NDIR)]
    ns = [lax.div(lengths[d], ms[d]) for d in range(NDIR)]
    phase = [lengths[d] - ns[d] * ms[d] for d in range(NDIR)]
    weight = [1.0 / (lengths[d].astype(jnp.float32)) * (1.0 / math.sqrt(E)) for d in range(NDIR)]
    q1 = [lax.div(ps[d], ms[d]) for d in range(NDIR)]
    r1 = [lax.div(ss[d], ms[d]) for d in range(NDIR)]
    q2 = [lax.div(2 * ps[d], ms[d]) for d in range(NDIR)]
    r2 = [lax.div(2 * ss[d], ms[d]) for d in range(NDIR)]
    three = [ms[d] == 3 for d in range(NDIR)]
    zero = jnp.zeros((8, 128), jnp.float32)

    def clear(b, _):
        s[b, pl.ds(ROWS, 8), :] = zero
        return 0
    lax.fori_loop(0, ZERO, clear, 0)
    s[ZERO] = jnp.zeros((PAD, 128), jnp.float32)
    for b in range(PLANES, ZERO):
        s[b] = jnp.zeros((PAD, 128), jnp.float32)
    for d in range(NDIR):
        for k in range(4):
            ds[d][k] = jnp.zeros((PAD, 128), jnp.float32)

    la = lane_iota((128, 128), 0)
    ll = lane_iota((128, 128), 1)
    same = (la & 3) == (ll >> 5)
    def make(qi, _):
        hit = same & (((la >> 2) ^ (ll & 31)) == qi)
        perm[qi] = jnp.where(hit, 1.0, 0.0).astype(jnp.bfloat16)
        return 0
    lax.fori_loop(0, B, make, 0)

    ri = lane_iota((256, 256), 0)
    ci = lane_iota((256, 256), 1)
    turn = jnp.where(((ri >> 3) == (ci & 31)) & ((ri & 7) == (ci >> 5)), 1.0, 0.0).astype(jnp.bfloat16)
    for k in range(parts):
        copies[k].wait()
        def two(t, _):
            base = pl.multiple_of(k * part + t * 512, 512)
            x = jnp.dot(turn, gv[pl.ds(base, 256), :], preferred_element_type=jnp.float32).reshape(B, 8, E)
            y = jnp.dot(turn, gv[pl.ds(base + 256, 256), :], preferred_element_type=jnp.float32).reshape(B, 8, E)
            z = jnp.concatenate([x, y], axis=1).astype(jnp.bfloat16)
            rb[pl.ds(0, B), pl.ds(pl.multiple_of((k * part // 512 + t) * 16, 16), 16), :] = z
            return 0
        lax.fori_loop(0, part // 512, two, 0)
    def dots(t, _):
        w = rb[pl.ds(2 * t, 2)].reshape(256, E)
        v = lax.dot_general(qx[...], w, (((1,), (1,)), ((), ())), preferred_element_type=jnp.float32)
        s[2 * t, pl.ds(0, ROWS), :] = v[:, :128]
        s[2 * t + 1, pl.ds(0, ROWS), :] = v[:, 128:]
        return 0
    lax.fori_loop(0, B // 2, dots, 0)
    hi = lane_iota((128, 160), 0)
    hj = lane_iota((128, 160), 1)
    def halo(t, _):
        ws = []
        for u in range(2):
            x = 2 * t + u
            pick = jnp.where((hj == hi + 1) & (hi < 127) | (hi == 127) & (hj == 128 + x), 1.0, 0.0).astype(jnp.bfloat16)
            src = jnp.concatenate([rb[x], rhv], axis=0)
            ws.append(jnp.dot(pick, src, preferred_element_type=jnp.float32).astype(jnp.bfloat16))
        w = jnp.concatenate(ws, axis=0)
        v = lax.dot_general(qx[...], w, (((1,), (1,)), ((), ())), preferred_element_type=jnp.float32)
        s[B + 2 * t, pl.ds(0, ROWS), :] = v[:, :128]
        s[B + 2 * t + 1, pl.ds(0, ROWS), :] = v[:, 128:]
        return 0
    lax.fori_loop(0, HALO // 2, halo, 0)

    def step(d, b, row, count, s0):
        dp = ds[d][(b + ss[d]) & 3, pl.ds(row + ps[d], count), :]
        t2 = s[jnp.where(three[d], b + r2[d], ZERO), pl.ds(row + q2[d], count), :]
        t1 = s[b + r1[d], pl.ds(row + q1[d], count), :]
        x2 = dp + t2
        x1 = x2 + t1
        x0 = x1 + s0
        e = jnp.where(phase[d] == 0, x0, jnp.where(phase[d] == 1, x1, x2))
        return x0, e

    for d in range(NDIR):
        last = B - 1 + ns[d] * ss[d]
        def plane(k, _):
            b = last - k
            for r in range(0, ROWS, SUPER):
                s0 = s[b, pl.ds(r, SUPER), :]
                x0, e = step(d, b, r, SUPER, s0)
                ds[d][b & 3, pl.ds(r, SUPER), :] = x0
                es[d][b & 31, pl.ds(r, SUPER), :] = e
            return 0
        lax.fori_loop(0, last - (B - 1), plane, 0)

    def final(k, _):
        b = B - 1 - k
        for r in range(0, ROWS, SUPER):
            s0 = s[b, pl.ds(r, SUPER), :]
            best = None
            for d in range(NDIR):
                x0, e = step(d, b, r, SUPER, s0)
                ds[d][b & 3, pl.ds(r, SUPER), :] = x0
                es[d][b & 31, pl.ds(r, SUPER), :] = e
                if r < rows:
                    en = es[d][(b + ns[d] * ss[d]) & 31, pl.ds(r + ns[d] * ps[d], SUPER), :]
                    v = (x0 - en) * weight[d]
                    best = v if best is None else jnp.maximum(best, v)
            if r < rows:
                o[b, pl.ds(r, SUPER), :] = best.astype(jnp.bfloat16)
        return 0
    lax.fori_loop(0, B, final, 0)

    lane = lane_iota((16, 128), 1)
    def network(x, bits):
        for t in range(5):
            mask = ((lane >> (bits + t)) & 1) == 1
            x = [jnp.where(mask, x[q ^ (1 << t)], x[q]) for q in range(B)]
        return x
    def skew(i, _):
        r = pl.ds(pl.multiple_of(i * 16, 16), 16)
        x = network([o[q, r, :] for q in range(B)], 2)
        for q in range(B):
            o[q, r, :] = x[q]
        return 0
    lax.fori_loop(0, rows // 16, skew, 0)
    def turn_lanes(qi, _):
        o[qi] = jnp.dot(o[qi], perm[qi], preferred_element_type=jnp.float32).astype(jnp.bfloat16)
        return 0
    lax.fori_loop(0, B, turn_lanes, 0)
    def back(i, _):
        r = pl.ds(pl.multiple_of(i * 16, 16), 16)
        x = network([o[q, r, :] for q in range(B)], 0)
        for q in range(B):
            osb[r, q * 128:(q + 1) * 128] = x[q]
        return 0
    lax.fori_loop(0, rows // 16, back, 0)
    c = pltpu.make_async_copy(osb, out_ref, osem)
    c.start()
    c.wait()


def call_compute(ratios, lengths, q, qh, rh, g):
    rows, cols = q.shape[0], g.shape[0]
    f32, bf = jnp.float32, jnp.bfloat16
    V = pltpu.VMEM
    return pl.pallas_call(
        compute,
        out_shape=jax.ShapeDtypeStruct((rows, cols), bf),
        in_specs=[pl.BlockSpec(memory_space=pltpu.SMEM)] * 2 + [pl.BlockSpec(memory_space=V)] * 3 + [pl.BlockSpec(memory_space=pl.ANY)],
        out_specs=pl.BlockSpec(memory_space=pl.ANY),
        scratch_shapes=[V((cols, E), bf), V((ROWS, E), bf), V((B, 128, E), bf), V((ZERO + 1, PAD, 128), f32)]
        + [V((4, PAD, 128), f32)] * 4 + [V((32, PAD, 128), f32)] * 4
        + [V((B, rows, 128), bf), V((B, 128, 128), bf), V((rows, cols), bf), pltpu.SemaphoreType.DMA((4,)), pltpu.SemaphoreType.DMA],
        compiler_params=pltpu.CompilerParams(vmem_limit_bytes=60 * 1024 * 1024),
        name="smooth",
    )(ratios, lengths, q, qh, rh, g)


def per_device(queries, references, ratios, lengths):
    g, qh, rh = call_gather(queries, references)
    return call_compute(ratios, lengths, queries, qh, rh, g)


def solution(mesh):
    placed = (P("pb", None), P("row", "pb", None), P(), P())
    return jax.shard_map(
        per_device, mesh=mesh, in_specs=placed, out_specs=P("pb", "row"), check_vma=False
    )
```

```python
import math

import jax
import jax.numpy as jnp
from jax import lax
from jax.experimental import pallas as pl
from jax.experimental.pallas import tpu as pltpu
from jax.sharding import PartitionSpec as P

E = 512
NDIR = 4
B = 32
HALO = 24
PLANES = B + HALO
ZERO = 58
TAIL = 32
PAD = 8
SUPER = 32
GROUP = 8
MESH = pl.DeviceIdType.MESH
F32, BF = jnp.float32, jnp.bfloat16


def iota(shape, d):
    return lax.broadcasted_iota(jnp.int32, shape, d)


def gather_and_smooth(steps_ref, lengths, q_ref, r_ref, o_ref,
                      gv, qx, rb, s, d0, d1, d2, d3, e0, e1, e2, e3, o,
                      local, ysem, u1, v1, far, v2, sib, qsem, hsem, osem):
    rows = q_ref.shape[0]
    all_rows = rows + TAIL
    ds, es = (d0, d1, d2, d3), (e0, e1, e2, e3)
    pb, row = lax.axis_index("pb"), lax.axis_index("row")
    c, y, x, z = pb & 1, (pb >> 1) & 1, (pb >> 2) & 3, pb >> 4
    last = pb == 63
    me = (z, x)

    def at(zx, y_, c_):
        return ((zx[0] * 4 + zx[1]) * 2 + y_) * 2 + c_

    def place(h, k):
        return (z, (x + k) & 3) if h == 0 else ((z + k) & 3, x)

    def spot(h, k1, k2):
        return ((z + k2) & 3, (x + k1) & 3) if h == 0 else ((z + k1) & 3, (x + k2) & 3)

    other_y, other_c = at(me, 1 - y, c), at(me, y, 1 - c)

    bar = pltpu.get_barrier_semaphore()
    peers = [other_y, other_c] + [at(place(h, k), y_, c) for h in range(2) for k in (1, 2, 3) for y_ in (0, 1)]
    for dev in peers:
        pl.semaphore_signal(bar, inc=1, device_id={"pb": dev}, device_id_type=MESH)

    @pl.when(pb < 63)
    def _():
        pl.semaphore_signal(bar, inc=1, device_id={"pb": pb + 1}, device_id_type=MESH)

    @pl.when(row == 0)
    def _():
        pl.semaphore_signal(bar, inc=1, device_id={"pb": at((0, x), y, 0), "row": 1}, device_id_type=MESH)

    heads = jnp.where((row == 1) & (z == 0) & (c == 0), 8, 0)
    pl.semaphore_wait(bar, len(peers) + jnp.minimum(pb, 1) + heads)

    sends = []

    def send(src, dst, sems, k, dev):
        copy = pltpu.make_async_remote_copy(src_ref=src, dst_ref=dst, send_sem=sems.at[0, k], recv_sem=sems.at[1, k],
                                            device_id={"pb": dev}, device_id_type=MESH)
        copy.start()
        sends.append(copy)

    def arrived(dst, sems, k):
        pltpu.make_async_copy(dst, dst, sems.at[1, k]).wait()

    def block(zx, y_, c_, lo, size):
        return gv.at[(zx[0] * 4 + zx[1]) * 2 + y_, pl.ds(c_ * 64 + lo, size)]

    def pair(zx, c_, lo, size):
        return gv.at[pl.ds((zx[0] * 4 + zx[1]) * 2, 2), pl.ds(c_ * 64 + lo, size)]

    own = r_ref.at[0]
    keep = pltpu.make_async_copy(own, block(me, y, c, 0, 64), local.at[0])
    keep.start()
    send(own, block(me, y, c, 0, 64), ysem, 0, other_y)
    for k in (1, 3, 2):
        for h in range(2):
            for w in range(2):
                y_ = y if w == 0 else 1 - y
                send(r_ref.at[0, pl.ds(32 * h, 32)], block(me, y, c, 32 * h, 32), u1, h * 6 + (k - 1) * 2 + w, at(place(h, k), y_, c))
    send(own, block(me, y, c, 0, 64), sib, 0, other_c)
    first = pltpu.make_async_remote_copy(src_ref=q_ref.at[pl.ds(0, TAIL)], dst_ref=qx.at[pl.ds(rows, TAIL)], send_sem=qsem.at[0],
                                         recv_sem=qsem.at[1], device_id={"pb": jnp.maximum(pb - 1, 0)}, device_id_type=MESH)

    @pl.when(pb > 0)
    def _():
        first.start()

    mine = pltpu.make_async_copy(q_ref, qx.at[pl.ds(0, rows)], local.at[1])
    mine.start()

    none = jnp.zeros((TAIL, E), BF)

    @pl.when(last)
    def _():
        qx[pl.ds(rows, TAIL), :] = none

    @pl.when(row == 1)
    def _():
        gv[32, pl.ds(0, TAIL), :] = none

    zero = jnp.zeros((PAD, 128), F32)

    def clear(b, _):
        s[b, pl.ds(all_rows, PAD), :] = zero
        return 0
    lax.fori_loop(0, PLANES, clear, 0)
    for b in range(PLANES, ZERO + 1):
        s[b] = jnp.zeros((all_rows + PAD, 128), F32)
    for d in range(NDIR):
        for k in range(4):
            ds[d][k] = jnp.zeros((all_rows + PAD, 128), F32)

    ri = iota((256, 256), 0)
    ci = iota((256, 256), 1)
    turn = jnp.where(((ri >> 3) == (ci & 31)) & ((ri & 7) == (ci >> 5)), 1.0, 0.0).astype(BF)

    def rearrange(chunk, shifted):
        k0 = 4 * chunk
        got = []
        for u in range(2):
            k = k0 + 2 * u
            if shifted:
                v = jnp.concatenate([gv[k, pl.ds(32, 96), :], gv[k + 1], gv[k + 2, pl.ds(0, 32), :]], axis=0)
            else:
                v = gv[pl.ds(k, 2)].reshape(256, E)
            planes = HALO if shifted else B
            got.append(jnp.dot(turn[:planes * 8], v, preferred_element_type=F32).reshape(planes, 8, E))
        lanes = pl.ds(pl.multiple_of(chunk * 16, 16), 16)
        rb[pl.ds(B if shifted else 0, got[0].shape[0]), lanes, :] = jnp.concatenate(got, axis=1).astype(BF)

    def slab(z_):
        def body(t, _):
            rearrange(2 * z_ + t, False)
            return 0
        lax.fori_loop(0, 2, body, 0)
        rearrange(2 * z_, True)

    steps = (0, 3, 1, 2)

    def onward(h, j, w, src, dst):
        send(src, dst, v1, w * 16 + h * 8 + 2 * j, at(spot(h, 0, 1), y, c))
        send(src, dst, v1, w * 16 + h * 8 + 2 * j + 1, at(spot(h, 0, 3), y, c))
        if w:
            send(src, dst, far, h * 4 + j, at(spot(h, 0, 2), y, c))

    for h in range(2):
        onward(h, 0, 0, r_ref.at[0, pl.ds(32 * h, 32)], block(me, y, c, 32 * h, 32))
    for j, k1 in enumerate(steps):
        for h in range(2):
            if k1:
                p = block(place(h, k1), y, c, 32 * h, 32)
                arrived(p, u1, h * 6 + (3 - k1) * 2)
                onward(h, j, 0, p, p)
    n = 2
    for j, k1 in enumerate(steps):
        if not k1:
            arrived(block(me, 1 - y, c, 0, 64), ysem, 0)
        for h in range(2):
            p = block(place(h, k1), 1 - y, c, 32 * h, 32)
            if k1:
                arrived(p, u1, h * 6 + (3 - k1) * 2 + 1)
            onward(h, j, 1, p, p)
            if k1:
                both = pair(place(h, k1), c, 32 * h, 32)
                send(both, both, sib, n, other_c)
                n += 1
    theirs = block(me, 1 - y, c, 0, 64)
    send(theirs, theirs, sib, 1, other_c)

    keep.wait()
    head = [pltpu.make_async_remote_copy(src_ref=gv.at[0, pl.ds(0, TAIL)], dst_ref=gv.at[32, pl.ds(0, TAIL)], send_sem=hsem.at[k],
                                         recv_sem=hsem.at[8], device_id={"pb": at((k >> 1, x), y, k & 1), "row": 0}, device_id_type=MESH)
            for k in range(8)]

    @pl.when((row == 1) & (z == 0) & (c == 0))
    def _():
        for copy in head:
            copy.start()

    for j, k1 in enumerate(steps):
        for h in range(2):
            for side, k2 in ((0, 3), (1, 1)):
                src = spot(h, k1, k2)
                arrived(block(src, y, c, 32 * h, 32), v1, h * 8 + 2 * j + side)
                piece = block(src, y, c, 32 * h + 16 * side, 16)
                send(piece, piece, v2, h * 8 + 2 * j + side, at(spot(h, 0, 1 if side == 0 else 3), y, c))
    for j, k1 in enumerate(steps):
        for h in range(2):
            for side, k2 in ((0, 3), (1, 1)):
                src = spot(h, k1, k2)
                arrived(block(src, 1 - y, c, 32 * h, 32), v1, 16 + h * 8 + 2 * j + side)
                both = pair(src, c, 32 * h, 32)
                send(both, both, sib, n, other_c)
                n += 1
    for j, k1 in enumerate(steps):
        for h in range(2):
            src = spot(h, k1, 2)
            for side in range(2):
                arrived(block(src, y, c, 32 * h + 16 * side, 16), v2, h * 8 + 2 * j + side)
            arrived(block(src, 1 - y, c, 32 * h, 32), far, h * 4 + j)
            both = pair(src, c, 32 * h, 32)
            send(both, both, sib, n, other_c)
            n += 1
    oc = 1 - c
    arrived(block(me, y, oc, 0, 64), sib, 0)
    arrived(block(me, 1 - y, oc, 0, 64), sib, 1)
    n = 2
    for k1 in steps[1:]:
        for h in range(2):
            arrived(pair(spot(h, k1, 0), oc, 32 * h, 32), sib, n)
            n += 1
    for k1 in steps:
        for h in range(2):
            for k2 in (3, 1):
                arrived(pair(spot(h, k1, k2), oc, 32 * h, 32), sib, n)
                n += 1
    for k1 in steps:
        for h in range(2):
            arrived(pair(spot(h, k1, 2), oc, 32 * h, 32), sib, n)
            n += 1
    for k in range(4):
        slab(k)

    @pl.when(row == 0)
    def _():
        head[0].wait_recv()

    @pl.when(pb < 63)
    def _():
        first.wait_recv()
    mine.wait()

    def edges(t, _):
        rearrange(2 * t + 1, True)
        return 0
    lax.fori_loop(0, 4, edges, 0)

    def dots(t, _):
        w = rb[pl.ds(GROUP * t, GROUP)].reshape(GROUP * 128, E)
        v = lax.dot_general(qx[...], w, (((1,), (1,)), ((), ())), preferred_element_type=F32)
        for u in range(GROUP):
            s[GROUP * t + u, pl.ds(0, all_rows), :] = v[:, u * 128:(u + 1) * 128]
        return 0
    lax.fori_loop(0, PLANES // GROUP, dots, 0)

    ps = [steps_ref[0, d] for d in range(NDIR)]
    ss = [steps_ref[1, d] for d in range(NDIR)]
    three = [jnp.maximum(ps[d], ss[d]) == 3 for d in range(NDIR)]
    ns = [jnp.where(three[d], lengths[d] // 3, lengths[d] // 2) for d in range(NDIR)]
    phase = [lengths[d] - ns[d] * jnp.where(three[d], 3, 2) for d in range(NDIR)]
    weight = [1.0 / (lengths[d].astype(F32)) * (1.0 / math.sqrt(E)) for d in range(NDIR)]

    def tap(v, other, times):
        return jnp.where(v > other, times, jnp.where(times * v >= other, 1, 0))
    q1 = [tap(ps[d], ss[d], 1) for d in range(NDIR)]
    r1 = [tap(ss[d], ps[d], 1) for d in range(NDIR)]
    q2 = [tap(ps[d], ss[d], 2) for d in range(NDIR)]
    r2 = [tap(ss[d], ps[d], 2) for d in range(NDIR)]

    def step(d, b, r, s0):
        dp = ds[d][(b + ss[d]) & 3, pl.ds(r + ps[d], SUPER), :]
        t2 = s[jnp.where(three[d], b + r2[d], ZERO), pl.ds(r + q2[d], SUPER), :]
        t1 = s[b + r1[d], pl.ds(r + q1[d], SUPER), :]
        x2 = dp + t2
        x1 = x2 + t1
        x0 = x1 + s0
        e = jnp.where(phase[d] == 0, x0, jnp.where(phase[d] == 1, x1, x2))
        ds[d][b & 3, pl.ds(r, SUPER), :] = x0
        es[d][b & 31, pl.ds(r, SUPER), :] = e
        return x0

    def past(k, _):
        b = PLANES - 1 - k
        for r in range(0, all_rows, SUPER):
            s0 = s[b, pl.ds(r, SUPER), :]
            for d in range(NDIR):
                step(d, b, r, s0)
        return 0
    lax.fori_loop(0, HALO, past, 0)

    def inside(k, _):
        b = B - 1 - k
        for r in range(0, all_rows, SUPER):
            s0 = s[b, pl.ds(r, SUPER), :]
            best = None
            for d in range(NDIR):
                x0 = step(d, b, r, s0)
                if r < rows:
                    en = es[d][(b + ns[d] * ss[d]) & 31, pl.ds(r + ns[d] * ps[d], SUPER), :]
                    v = (x0 - en) * weight[d]
                    best = v if best is None else jnp.maximum(best, v)
            if r < rows:
                o[b, pl.ds(r, SUPER), :] = best.astype(BF)
        return 0
    outs = []
    for k in range(4):
        lax.fori_loop(8 * k, 8 * k + 8, inside, 0)
        part = pl.ds(B - 8 * k - 8, 8)
        copy = pltpu.make_async_copy(o.at[part], o_ref.at[part], osem.at[k])
        copy.start()
        outs.append(copy)
    for copy in sends:
        copy.wait_send()

    @pl.when(pb > 0)
    def _():
        first.wait_send()

    @pl.when((row == 1) & (z == 0) & (c == 0))
    def _():
        for copy in head:
            copy.wait_send()
    for copy in outs:
        copy.wait()


def untangle(o_ref, out_ref, o, perm, flat, isem, osem):
    rows = o_ref.shape[1]
    parts = 2
    size = rows // parts
    ins = [pltpu.make_async_copy(o_ref.at[:, pl.ds(k * size, size)], o.at[:, pl.ds(k * size, size)], isem.at[k]) for k in range(parts)]
    for copy in ins:
        copy.start()
    la = iota((128, 128), 0)
    ll = iota((128, 128), 1)
    same = (la & 3) == (ll >> 5)

    def make(q, _):
        perm[q] = jnp.where(same & (((la >> 2) ^ (ll & 31)) == q), 1.0, 0.0).astype(BF)
        return 0
    lax.fori_loop(0, B, make, 0)
    lane = iota((16, 128), 1)
    bit = [((lane >> t) & 1).astype(F32).astype(BF) for t in range(7)]

    def network(v, bits):
        for t in range(5):
            mask = bit[bits + t] > 0.5
            v = [jnp.where(mask, v[q ^ (1 << t)], v[q]) for q in range(B)]
        return v
    outs = []
    for k in range(parts):
        ins[k].wait()

        def skew(i, _):
            r = pl.ds(pl.multiple_of(k * size + i * 16, 16), 16)
            v = network([o[q, r, :] for q in range(B)], 2)
            for q in range(B):
                o[q, r, :] = v[q]
            return 0
        lax.fori_loop(0, size // 16, skew, 0)

        def lanes(t, _):
            r = pl.ds(k * size, size)
            got = [jnp.dot(o[8 * t + u, r, :], perm[8 * t + u], preferred_element_type=F32).astype(BF) for u in range(8)]
            for u in range(8):
                o[8 * t + u, r, :] = got[u]
            return 0
        lax.fori_loop(0, B // 8, lanes, 0)

        def back(i, _):
            r = pl.ds(pl.multiple_of(k * size + i * 16, 16), 16)
            v = network([o[q, r, :] for q in range(B)], 0)
            for q in range(B):
                flat[r, q * 128:(q + 1) * 128] = v[q]
            return 0
        lax.fori_loop(0, size // 16, back, 0)
        part = pl.ds(k * size, size)
        copy = pltpu.make_async_copy(flat.at[part], out_ref.at[part], osem.at[k])
        copy.start()
        outs.append(copy)
    for copy in outs:
        copy.wait()


def per_device(queries, references, ratios, lengths):
    rows = queries.shape[0]
    cols = references.shape[1] * 64
    V, D, ANY = pltpu.VMEM, pltpu.SemaphoreType.DMA, pl.BlockSpec(memory_space=pl.ANY)
    all_rows = rows + TAIL
    o = pl.pallas_call(
        gather_and_smooth,
        out_shape=jax.ShapeDtypeStruct((B, rows, 128), BF),
        in_specs=[pl.BlockSpec(memory_space=pltpu.SMEM)] * 2 + [ANY] * 2,
        out_specs=ANY,
        scratch_shapes=[V((33, 128, E), BF), V((all_rows, E), BF), V((PLANES, 128, E), BF), V((ZERO + 1, all_rows + PAD, 128), F32)]
        + [V((4, all_rows + PAD, 128), F32)] * 4 + [V((32, all_rows + PAD, 128), F32)] * 4 + [V((B, rows, 128), BF)]
        + [D((2,)), D((2, 1)), D((2, 12)), D((2, 32)), D((2, 8)), D((2, 16)), D((2, 32)), D((2,)), D((9,)), D((4,))],
        compiler_params=pltpu.CompilerParams(collective_id=0, has_side_effects=True, vmem_limit_bytes=60 * 1024 * 1024),
        name="gather_and_smooth",
    )(ratios.T, lengths, queries, references)
    return pl.pallas_call(
        untangle,
        out_shape=jax.ShapeDtypeStruct((rows, cols), BF),
        in_specs=[ANY],
        out_specs=ANY,
        scratch_shapes=[V((B, rows, 128), BF), V((B, 128, 128), BF), V((rows, cols), BF), D((2,)), D((2,))],
        compiler_params=pltpu.CompilerParams(vmem_limit_bytes=60 * 1024 * 1024),
        name="untangle",
    )(o)


def solution(mesh):
    placed = (P("pb", None), P("row", "pb", None), P(), P())
    return jax.shard_map(
        per_device, mesh=mesh, in_specs=placed, out_specs=P("pb", "row"), check_vma=False
    )
```

```python
import math

import jax
import jax.numpy as jnp
from jax import lax
from jax.experimental import pallas as pl
from jax.experimental.pallas import tpu as pltpu
from jax.sharding import PartitionSpec as P

E = 512
NDIR = 4
B = 32
HALO = 24
PLANES = B + HALO
ZERO = 58
TAIL = 32
PAD = 8
SUPER = 32
GROUP = 28
MESH = pl.DeviceIdType.MESH
F32, BF = jnp.float32, jnp.bfloat16


def iota(shape, d):
    return lax.broadcasted_iota(jnp.int32, shape, d)


def gather_and_smooth(steps_ref, lengths, q_ref, r_ref, o_ref,
                      gv, qx, rb, s, d0, d1, d2, d3, e0, e1, e2, e3, o,
                      local, ysem, u1, v1, far, v2, sib, qsem, hsem, osem):
    rows = q_ref.shape[0]
    all_rows = rows + TAIL
    ds, es = (d0, d1, d2, d3), (e0, e1, e2, e3)
    pb, row = lax.axis_index("pb"), lax.axis_index("row")
    c, y, x, z = pb & 1, (pb >> 1) & 1, (pb >> 2) & 3, pb >> 4
    last = pb == 63
    me = (z, x)

    def at(zx, y_, c_):
        return ((zx[0] * 4 + zx[1]) * 2 + y_) * 2 + c_

    def place(h, k):
        return (z, (x + k) & 3) if h == 0 else ((z + k) & 3, x)

    def spot(h, k1, k2):
        return ((z + k2) & 3, (x + k1) & 3) if h == 0 else ((z + k1) & 3, (x + k2) & 3)

    other_y, other_c = at(me, 1 - y, c), at(me, y, 1 - c)

    bar = pltpu.get_barrier_semaphore()
    peers = [other_y, other_c] + [at(place(h, k), y_, c) for h in range(2) for k in (1, 2, 3) for y_ in (0, 1)]
    for dev in peers:
        pl.semaphore_signal(bar, inc=1, device_id={"pb": dev}, device_id_type=MESH)

    @pl.when(pb < 63)
    def _():
        pl.semaphore_signal(bar, inc=1, device_id={"pb": pb + 1}, device_id_type=MESH)

    @pl.when(row == 0)
    def _():
        pl.semaphore_signal(bar, inc=1, device_id={"pb": at((0, x), y, 0), "row": 1}, device_id_type=MESH)

    heads = jnp.where((row == 1) & (z == 0) & (c == 0), 8, 0)
    pl.semaphore_wait(bar, len(peers) + jnp.minimum(pb, 1) + heads)

    sends = []

    def send(src, dst, sems, k, dev):
        copy = pltpu.make_async_remote_copy(src_ref=src, dst_ref=dst, send_sem=sems.at[0, k], recv_sem=sems.at[1, k],
                                            device_id={"pb": dev}, device_id_type=MESH)
        copy.start()
        sends.append(copy)

    def arrived(dst, sems, k):
        pltpu.make_async_copy(dst, dst, sems.at[1, k]).wait()

    def block(zx, y_, c_, lo, size):
        return gv.at[(zx[0] * 4 + zx[1]) * 2 + y_, pl.ds(c_ * 64 + lo, size)]

    def pair(zx, c_, lo, size):
        return gv.at[pl.ds((zx[0] * 4 + zx[1]) * 2, 2), pl.ds(c_ * 64 + lo, size)]

    own = r_ref.at[0]
    keep = pltpu.make_async_copy(own, block(me, y, c, 0, 64), local.at[0])
    keep.start()
    send(own, block(me, y, c, 0, 64), ysem, 0, other_y)
    for k in (1, 3, 2):
        for h in range(2):
            for w in range(2):
                y_ = y if w == 0 else 1 - y
                send(r_ref.at[0, pl.ds(32 * h, 32)], block(me, y, c, 32 * h, 32), u1, h * 6 + (k - 1) * 2 + w, at(place(h, k), y_, c))
    send(own, block(me, y, c, 0, 64), sib, 0, other_c)
    first = pltpu.make_async_remote_copy(src_ref=q_ref.at[pl.ds(0, TAIL)], dst_ref=qx.at[pl.ds(rows, TAIL)], send_sem=qsem.at[0],
                                         recv_sem=qsem.at[1], device_id={"pb": jnp.maximum(pb - 1, 0)}, device_id_type=MESH)

    @pl.when(pb > 0)
    def _():
        first.start()

    mine = pltpu.make_async_copy(q_ref, qx.at[pl.ds(0, rows)], local.at[1])
    mine.start()

    none = jnp.zeros((TAIL, E), BF)

    @pl.when(last)
    def _():
        qx[pl.ds(rows, TAIL), :] = none

    @pl.when(row == 1)
    def _():
        gv[32, pl.ds(0, TAIL), :] = none

    zero = jnp.zeros((PAD, 128), F32)

    def clear(b, _):
        s[b, pl.ds(all_rows, PAD), :] = zero
        return 0
    lax.fori_loop(0, PLANES, clear, 0)
    for b in range(PLANES, ZERO + 1):
        s[b] = jnp.zeros((all_rows + PAD, 128), F32)
    for d in range(NDIR):
        for k in range(4):
            ds[d][k] = jnp.zeros((all_rows + PAD, 128), F32)

    ri = iota((256, 256), 0)
    ci = iota((256, 256), 1)
    turn = jnp.where(((ri >> 3) == (ci & 31)) & ((ri & 7) == (ci >> 5)), 1.0, 0.0).astype(BF)

    def rearrange(h, group, shifted):
        got = []
        for u in range(2):
            rows_of = []
            for i in range(4):
                hi, y_ = 2 * u + (i >> 1), i & 1
                k = (8 * group + 2 * hi if h == 0 else 8 * hi + 2 * group) + y_
                for core in range(2):
                    if not shifted:
                        part = gv[k, pl.ds(64 * core + 32 * h, 32), :]
                    elif h == 0:
                        part = gv[k, pl.ds(64 * core + 32, 32), :]
                    elif core == 0:
                        part = gv[k, pl.ds(64, 32), :]
                    else:
                        part = gv[k + 1, pl.ds(0, 32), :]
                    rows_of.append(part)
            planes = HALO if shifted else B
            got.append(jnp.dot(turn[:planes * 8], jnp.concatenate(rows_of, axis=0), preferred_element_type=F32).reshape(planes, 8, E))
        lanes = pl.ds(pl.multiple_of(64 * h + group * 16, 16), 16)
        rb[pl.ds(B if shifted else 0, got[0].shape[0]), lanes, :] = jnp.concatenate(got, axis=1).astype(BF)

    steps = (0, 3, 1, 2)

    def onward(h, j, w, src, dst):
        send(src, dst, v1, w * 16 + h * 8 + 2 * j, at(spot(h, 0, 1), y, c))
        send(src, dst, v1, w * 16 + h * 8 + 2 * j + 1, at(spot(h, 0, 3), y, c))
        if w:
            send(src, dst, far, h * 4 + j, at(spot(h, 0, 2), y, c))

    for h in range(2):
        onward(h, 0, 0, r_ref.at[0, pl.ds(32 * h, 32)], block(me, y, c, 32 * h, 32))
    for j, k1 in enumerate(steps):
        for h in range(2):
            if k1:
                p = block(place(h, k1), y, c, 32 * h, 32)
                arrived(p, u1, h * 6 + (3 - k1) * 2)
                onward(h, j, 0, p, p)
    n = 2
    for j, k1 in enumerate(steps):
        if not k1:
            arrived(block(me, 1 - y, c, 0, 64), ysem, 0)
        for h in range(2):
            p = block(place(h, k1), 1 - y, c, 32 * h, 32)
            if k1:
                arrived(p, u1, h * 6 + (3 - k1) * 2 + 1)
            onward(h, j, 1, p, p)
            if k1:
                both = pair(place(h, k1), c, 32 * h, 32)
                send(both, both, sib, n, other_c)
                n += 1
    theirs = block(me, 1 - y, c, 0, 64)
    send(theirs, theirs, sib, 1, other_c)

    keep.wait()
    head = [pltpu.make_async_remote_copy(src_ref=gv.at[0, pl.ds(0, TAIL)], dst_ref=gv.at[32, pl.ds(0, TAIL)], send_sem=hsem.at[k],
                                         recv_sem=hsem.at[8], device_id={"pb": at((k >> 1, x), y, k & 1), "row": 0}, device_id_type=MESH)
            for k in range(8)]

    @pl.when((row == 1) & (z == 0) & (c == 0))
    def _():
        for copy in head:
            copy.start()

    for j, k1 in enumerate(steps):
        for h in range(2):
            for side, k2 in ((0, 3), (1, 1)):
                src = spot(h, k1, k2)
                arrived(block(src, y, c, 32 * h, 32), v1, h * 8 + 2 * j + side)
                piece = block(src, y, c, 32 * h + 16 * side, 16)
                send(piece, piece, v2, h * 8 + 2 * j + side, at(spot(h, 0, 1 if side == 0 else 3), y, c))
    for j, k1 in enumerate(steps):
        for h in range(2):
            for side, k2 in ((0, 3), (1, 1)):
                src = spot(h, k1, k2)
                arrived(block(src, 1 - y, c, 32 * h, 32), v1, 16 + h * 8 + 2 * j + side)
                both = pair(src, c, 32 * h, 32)
                send(both, both, sib, n, other_c)
                n += 1
    oc = 1 - c
    arrived(block(me, y, oc, 0, 64), sib, 0)
    arrived(block(me, 1 - y, oc, 0, 64), sib, 1)
    n2 = 2
    for k1 in steps[1:]:
        for h in range(2):
            arrived(pair(place(h, k1), oc, 32 * h, 32), sib, n2)
            n2 += 1
    rearrange(0, z, False)
    rearrange(1, x, False)
    for k1 in steps:
        for h in range(2):
            for k2 in (3, 1):
                arrived(pair(spot(h, k1, k2), oc, 32 * h, 32), sib, n2)
                n2 += 1
    for k in (3, 1):
        rearrange(0, (z + k) & 3, False)
        rearrange(1, (x + k) & 3, False)
    for j, k1 in enumerate(steps):
        for h in range(2):
            src = spot(h, k1, 2)
            for side in range(2):
                arrived(block(src, y, c, 32 * h + 16 * side, 16), v2, h * 8 + 2 * j + side)
            arrived(block(src, 1 - y, c, 32 * h, 32), far, h * 4 + j)
            both = pair(src, c, 32 * h, 32)
            send(both, both, sib, n, other_c)
            n += 1
    for k1 in steps:
        for h in range(2):
            arrived(pair(spot(h, k1, 2), oc, 32 * h, 32), sib, n2)
            n2 += 1
    rearrange(0, (z + 2) & 3, False)
    rearrange(1, (x + 2) & 3, False)

    @pl.when(row == 0)
    def _():
        head[0].wait_recv()

    @pl.when(pb < 63)
    def _():
        first.wait_recv()
    mine.wait()

    def edges(t, _):
        for h in range(2):
            rearrange(h, t, True)
        return 0
    lax.fori_loop(0, 4, edges, 0)

    def dots(t, _):
        w = rb[pl.ds(GROUP * t, GROUP)].reshape(GROUP * 128, E)
        v = lax.dot_general(qx[...], w, (((1,), (1,)), ((), ())), preferred_element_type=F32)
        for u in range(GROUP):
            s[GROUP * t + u, pl.ds(0, all_rows), :] = v[:, u * 128:(u + 1) * 128]
        return 0
    lax.fori_loop(0, PLANES // GROUP, dots, 0)

    ps = [steps_ref[0, d] for d in range(NDIR)]
    ss = [steps_ref[1, d] for d in range(NDIR)]
    three = [jnp.maximum(ps[d], ss[d]) == 3 for d in range(NDIR)]
    ns = [jnp.where(three[d], lengths[d] // 3, lengths[d] // 2) for d in range(NDIR)]
    phase = [lengths[d] - ns[d] * jnp.where(three[d], 3, 2) for d in range(NDIR)]
    weight = [1.0 / (lengths[d].astype(F32)) * (1.0 / math.sqrt(E)) for d in range(NDIR)]

    def tap(v, other, times):
        return jnp.where(v > other, times, jnp.where(times * v >= other, 1, 0))
    q1 = [tap(ps[d], ss[d], 1) for d in range(NDIR)]
    r1 = [tap(ss[d], ps[d], 1) for d in range(NDIR)]
    q2 = [tap(ps[d], ss[d], 2) for d in range(NDIR)]
    r2 = [tap(ss[d], ps[d], 2) for d in range(NDIR)]

    def step(d, b, r, s0):
        dp = ds[d][(b + ss[d]) & 3, pl.ds(r + ps[d], SUPER), :]
        t2 = s[jnp.where(three[d], b + r2[d], ZERO), pl.ds(r + q2[d], SUPER), :]
        t1 = s[b + r1[d], pl.ds(r + q1[d], SUPER), :]
        x2 = dp + t2
        x1 = x2 + t1
        x0 = x1 + s0
        e = jnp.where(phase[d] == 0, x0, jnp.where(phase[d] == 1, x1, x2))
        ds[d][b & 3, pl.ds(r, SUPER), :] = x0
        es[d][b & 31, pl.ds(r, SUPER), :] = e
        return x0

    def past(k, _):
        for b in (PLANES - 1 - 2 * k, PLANES - 2 - 2 * k):
            for r in range(0, all_rows, SUPER):
                s0 = s[b, pl.ds(r, SUPER), :]
                for d in range(NDIR):
                    step(d, b, r, s0)
        return 0
    lax.fori_loop(0, HALO // 2, past, 0)

    def inside(k, _):
        for b in (B - 1 - 2 * k, B - 2 - 2 * k):
            within(b)
        return 0

    def within(b):
        for r in range(0, all_rows, SUPER):
            s0 = s[b, pl.ds(r, SUPER), :]
            best = None
            for d in range(NDIR):
                x0 = step(d, b, r, s0)
                if r < rows:
                    en = es[d][(b + ns[d] * ss[d]) & 31, pl.ds(r + ns[d] * ps[d], SUPER), :]
                    v = (x0 - en) * weight[d]
                    best = v if best is None else jnp.maximum(best, v)
            if r < rows:
                o[b, pl.ds(r, SUPER), :] = best.astype(BF)
    outs = []
    for k in range(4):
        lax.fori_loop(4 * k, 4 * k + 4, inside, 0)
        part = pl.ds(B - 8 * k - 8, 8)
        copy = pltpu.make_async_copy(o.at[part], o_ref.at[part], osem.at[k])
        copy.start()
        outs.append(copy)
    for copy in sends:
        copy.wait_send()

    @pl.when(pb > 0)
    def _():
        first.wait_send()

    @pl.when((row == 1) & (z == 0) & (c == 0))
    def _():
        for copy in head:
            copy.wait_send()
    for copy in outs:
        copy.wait()


def untangle(o_ref, out_ref, o, perm, flat, isem, osem):
    rows = o_ref.shape[1]
    parts = 2
    size = rows // parts
    ins = [pltpu.make_async_copy(o_ref.at[:, pl.ds(k * size, size)], o.at[:, pl.ds(k * size, size)], isem.at[k]) for k in range(parts)]
    for copy in ins:
        copy.start()
    la = iota((128, 128), 0)
    ll = iota((128, 128), 1)

    def block_of(lane):
        n = lane & 63
        return jnp.where(lane < 64, n, ((n >> 2) & 3) * 16 + (n >> 4) * 4 + (n & 3))
    same = (block_of(la) & 1) * 2 + (la >> 6) == (ll >> 5)

    def make(q, _):
        perm[q] = jnp.where(same & (((block_of(la) >> 1) ^ (ll & 31)) == q), 1.0, 0.0).astype(BF)
        return 0
    lax.fori_loop(0, B, make, 0)
    lane = iota((16, 128), 1)
    bit = [[((v >> t) & 1).astype(F32).astype(BF) for t in range(5)] for v in (block_of(lane) >> 1, lane)]

    def network(v, way):
        for t in range(5):
            mask = bit[way][t] > 0.5
            v = [jnp.where(mask, v[q ^ (1 << t)], v[q]) for q in range(B)]
        return v
    outs = []
    for k in range(parts):
        ins[k].wait()

        def skew(i, _):
            r = pl.ds(pl.multiple_of(k * size + i * 16, 16), 16)
            v = network([o[q, r, :] for q in range(B)], 0)
            for q in range(B):
                o[q, r, :] = v[q]
            return 0
        lax.fori_loop(0, size // 16, skew, 0)

        def lanes(t, _):
            r = pl.ds(k * size, size)
            got = [jnp.dot(o[32 * t + u, r, :], perm[32 * t + u], preferred_element_type=F32).astype(BF) for u in range(32)]
            for u in range(32):
                o[32 * t + u, r, :] = got[u]
            return 0
        lax.fori_loop(0, B // 32, lanes, 0)

        def back(i, _):
            r = pl.ds(pl.multiple_of(k * size + i * 16, 16), 16)
            v = network([o[q, r, :] for q in range(B)], 1)
            for q in range(B):
                flat[r, q * 128:(q + 1) * 128] = v[q]
            return 0
        lax.fori_loop(0, size // 16, back, 0)
        part = pl.ds(k * size, size)
        copy = pltpu.make_async_copy(flat.at[part], out_ref.at[part], osem.at[k])
        copy.start()
        outs.append(copy)
    for copy in outs:
        copy.wait()


def per_device(queries, references, ratios, lengths):
    rows = queries.shape[0]
    cols = references.shape[1] * 64
    V, D, ANY = pltpu.VMEM, pltpu.SemaphoreType.DMA, pl.BlockSpec(memory_space=pl.ANY)
    all_rows = rows + TAIL
    o = pl.pallas_call(
        gather_and_smooth,
        out_shape=jax.ShapeDtypeStruct((B, rows, 128), BF),
        in_specs=[pl.BlockSpec(memory_space=pltpu.SMEM)] * 2 + [ANY] * 2,
        out_specs=ANY,
        scratch_shapes=[V((33, 128, E), BF), V((all_rows, E), BF), V((PLANES, 128, E), BF), V((ZERO + 1, all_rows + PAD, 128), F32)]
        + [V((4, all_rows + PAD, 128), F32)] * 4 + [V((32, all_rows + PAD, 128), F32)] * 4 + [V((B, rows, 128), BF)]
        + [D((2,)), D((2, 1)), D((2, 12)), D((2, 32)), D((2, 8)), D((2, 16)), D((2, 32)), D((2,)), D((9,)), D((4,))],
        compiler_params=pltpu.CompilerParams(collective_id=0, has_side_effects=True, vmem_limit_bytes=60 * 1024 * 1024),
        name="gather_and_smooth",
    )(ratios.T, lengths, queries, references)
    return pl.pallas_call(
        untangle,
        out_shape=jax.ShapeDtypeStruct((rows, cols), BF),
        in_specs=[ANY],
        out_specs=ANY,
        scratch_shapes=[V((B, rows, 128), BF), V((B, 128, 128), BF), V((rows, cols), BF), D((2,)), D((2,))],
        compiler_params=pltpu.CompilerParams(vmem_limit_bytes=60 * 1024 * 1024),
        name="untangle",
    )(o)


def solution(mesh):
    placed = (P("pb", None), P("row", "pb", None), P(), P())
    return jax.shard_map(
        per_device, mesh=mesh, in_specs=placed, out_specs=P("pb", "row"), check_vma=False
    )
```

```python
import math

import jax
import jax.numpy as jnp
from jax import lax
from jax.experimental import pallas as pl
from jax.experimental.pallas import tpu as pltpu
from jax.sharding import PartitionSpec as P

E = 512
NDIR = 4
B = 32
HALO = 24
PLANES = B + HALO
ZERO = 58
TAIL = 32
PAD = 8
SUPER = 32
GROUP = 56
MESH = pl.DeviceIdType.MESH
F32, BF = jnp.float32, jnp.bfloat16


def iota(shape, d):
    return lax.broadcasted_iota(jnp.int32, shape, d)


def gather_and_smooth(steps_ref, lengths, q_ref, r_ref, o_ref,
                      gv, qx, rb, s, d0, d1, d2, d3, e0, e1, e2, e3, o,
                      local, ysem, u1, v1, far, v2, sib, qsem, hsem, osem):
    rows = q_ref.shape[0]
    all_rows = rows + TAIL
    ds, es = (d0, d1, d2, d3), (e0, e1, e2, e3)
    pb, row = lax.axis_index("pb"), lax.axis_index("row")
    c, y, x, z = pb & 1, (pb >> 1) & 1, (pb >> 2) & 3, pb >> 4
    last = pb == 63
    me = (z, x)

    def at(zx, y_, c_):
        return ((zx[0] * 4 + zx[1]) * 2 + y_) * 2 + c_

    def place(h, k):
        return (z, (x + k) & 3) if h == 0 else ((z + k) & 3, x)

    def spot(h, k1, k2):
        return ((z + k2) & 3, (x + k1) & 3) if h == 0 else ((z + k1) & 3, (x + k2) & 3)

    other_y, other_c = at(me, 1 - y, c), at(me, y, 1 - c)

    bar = pltpu.get_barrier_semaphore()
    peers = [other_y, other_c] + [at(place(h, k), y_, c) for h in range(2) for k in (1, 2, 3) for y_ in (0, 1)]
    for dev in peers:
        pl.semaphore_signal(bar, inc=1, device_id={"pb": dev}, device_id_type=MESH)

    @pl.when(pb < 63)
    def _():
        pl.semaphore_signal(bar, inc=1, device_id={"pb": pb + 1}, device_id_type=MESH)

    @pl.when(row == 0)
    def _():
        pl.semaphore_signal(bar, inc=1, device_id={"pb": at((0, x), y, 0), "row": 1}, device_id_type=MESH)

    heads = jnp.where((row == 1) & (z == 0) & (c == 0), 8, 0)
    pl.semaphore_wait(bar, len(peers) + jnp.minimum(pb, 1) + heads)

    sends = []

    def send(src, dst, sems, k, dev):
        copy = pltpu.make_async_remote_copy(src_ref=src, dst_ref=dst, send_sem=sems.at[0, k], recv_sem=sems.at[1, k],
                                            device_id={"pb": dev}, device_id_type=MESH)
        copy.start()
        sends.append(copy)

    def arrived(dst, sems, k):
        pltpu.make_async_copy(dst, dst, sems.at[1, k]).wait()

    def block(zx, y_, c_, lo, size):
        return gv.at[(zx[0] * 4 + zx[1]) * 2 + y_, pl.ds(c_ * 64 + lo, size)]

    def pair(zx, c_, lo, size):
        return gv.at[pl.ds((zx[0] * 4 + zx[1]) * 2, 2), pl.ds(c_ * 64 + lo, size)]

    own = r_ref.at[0]
    keep = pltpu.make_async_copy(own, block(me, y, c, 0, 64), local.at[0])
    keep.start()
    send(own, block(me, y, c, 0, 64), ysem, 0, other_y)
    for k in (1, 3, 2):
        for h in range(2):
            for w in range(2):
                y_ = y if w == 0 else 1 - y
                send(r_ref.at[0, pl.ds(32 * h, 32)], block(me, y, c, 32 * h, 32), u1, h * 6 + (k - 1) * 2 + w, at(place(h, k), y_, c))
    send(own, block(me, y, c, 0, 64), sib, 0, other_c)
    first = pltpu.make_async_remote_copy(src_ref=q_ref.at[pl.ds(0, TAIL)], dst_ref=qx.at[pl.ds(rows, TAIL)], send_sem=qsem.at[0],
                                         recv_sem=qsem.at[1], device_id={"pb": jnp.maximum(pb - 1, 0)}, device_id_type=MESH)

    @pl.when(pb > 0)
    def _():
        first.start()

    mine = pltpu.make_async_copy(q_ref, qx.at[pl.ds(0, rows)], local.at[1])
    mine.start()

    none = jnp.zeros((TAIL, E), BF)

    @pl.when(last)
    def _():
        qx[pl.ds(rows, TAIL), :] = none

    @pl.when(row == 1)
    def _():
        gv[32, pl.ds(0, TAIL), :] = none

    zero = jnp.zeros((PAD, 128), F32)

    def clear(b, _):
        s[b, pl.ds(all_rows, PAD), :] = zero
        return 0
    lax.fori_loop(0, PLANES, clear, 0)
    for b in range(PLANES, ZERO + 1):
        s[b] = jnp.zeros((all_rows + PAD, 128), F32)
    for d in range(NDIR):
        for k in range(4):
            ds[d][k] = jnp.zeros((all_rows + PAD, 128), F32)

    ri = iota((256, 256), 0)
    ci = iota((256, 256), 1)
    turn = jnp.where(((ri >> 3) == (ci & 31)) & ((ri & 7) == (ci >> 5)), 1.0, 0.0).astype(BF)

    def rearrange(h, group, shifted):
        got = []
        for u in range(2):
            rows_of = []
            for i in range(4):
                hi, y_ = 2 * u + (i >> 1), i & 1
                k = (8 * group + 2 * hi if h == 0 else 8 * hi + 2 * group) + y_
                for core in range(2):
                    if not shifted:
                        part = gv[k, pl.ds(64 * core + 32 * h, 32), :]
                    elif h == 0:
                        part = gv[k, pl.ds(64 * core + 32, 32), :]
                    elif core == 0:
                        part = gv[k, pl.ds(64, 32), :]
                    else:
                        part = gv[k + 1, pl.ds(0, 32), :]
                    rows_of.append(part)
            planes = HALO if shifted else B
            got.append(jnp.dot(turn[:planes * 8], jnp.concatenate(rows_of, axis=0), preferred_element_type=F32).reshape(planes, 8, E))
        lanes = pl.ds(pl.multiple_of(64 * h + group * 16, 16), 16)
        rb[pl.ds(B if shifted else 0, got[0].shape[0]), lanes, :] = jnp.concatenate(got, axis=1).astype(BF)

    steps = (0, 3, 1, 2)

    def onward(h, j, w, src, dst):
        send(src, dst, v1, w * 16 + h * 8 + 2 * j, at(spot(h, 0, 1), y, c))
        send(src, dst, v1, w * 16 + h * 8 + 2 * j + 1, at(spot(h, 0, 3), y, c))
        if w:
            send(src, dst, far, h * 4 + j, at(spot(h, 0, 2), y, c))

    for h in range(2):
        onward(h, 0, 0, r_ref.at[0, pl.ds(32 * h, 32)], block(me, y, c, 32 * h, 32))
    for j, k1 in enumerate(steps):
        for h in range(2):
            if k1:
                p = block(place(h, k1), y, c, 32 * h, 32)
                arrived(p, u1, h * 6 + (3 - k1) * 2)
                onward(h, j, 0, p, p)
    n = 2
    for j, k1 in enumerate(steps):
        if not k1:
            arrived(block(me, 1 - y, c, 0, 64), ysem, 0)
        for h in range(2):
            p = block(place(h, k1), 1 - y, c, 32 * h, 32)
            if k1:
                arrived(p, u1, h * 6 + (3 - k1) * 2 + 1)
            onward(h, j, 1, p, p)
            if k1:
                both = pair(place(h, k1), c, 32 * h, 32)
                send(both, both, sib, n, other_c)
                n += 1
    theirs = block(me, 1 - y, c, 0, 64)
    send(theirs, theirs, sib, 1, other_c)

    keep.wait()
    head = [pltpu.make_async_remote_copy(src_ref=gv.at[0, pl.ds(0, TAIL)], dst_ref=gv.at[32, pl.ds(0, TAIL)], send_sem=hsem.at[k],
                                         recv_sem=hsem.at[8], device_id={"pb": at((k >> 1, x), y, k & 1), "row": 0}, device_id_type=MESH)
            for k in range(8)]

    @pl.when((row == 1) & (z == 0) & (c == 0))
    def _():
        for copy in head:
            copy.start()

    for j, k1 in enumerate(steps):
        for h in range(2):
            for side, k2 in ((0, 3), (1, 1)):
                src = spot(h, k1, k2)
                arrived(block(src, y, c, 32 * h, 32), v1, h * 8 + 2 * j + side)
                piece = block(src, y, c, 32 * h + 16 * side, 16)
                send(piece, piece, v2, h * 8 + 2 * j + side, at(spot(h, 0, 1 if side == 0 else 3), y, c))
    for j, k1 in enumerate(steps):
        for h in range(2):
            for side, k2 in ((0, 3), (1, 1)):
                src = spot(h, k1, k2)
                arrived(block(src, 1 - y, c, 32 * h, 32), v1, 16 + h * 8 + 2 * j + side)
                both = pair(src, c, 32 * h, 32)
                send(both, both, sib, n, other_c)
                n += 1
    oc = 1 - c
    arrived(block(me, y, oc, 0, 64), sib, 0)
    arrived(block(me, 1 - y, oc, 0, 64), sib, 1)
    n2 = 2
    for k1 in steps[1:]:
        for h in range(2):
            arrived(pair(place(h, k1), oc, 32 * h, 32), sib, n2)
            n2 += 1
    rearrange(0, z, False)
    rearrange(1, x, False)
    for k1 in steps:
        for h in range(2):
            for k2 in (3, 1):
                arrived(pair(spot(h, k1, k2), oc, 32 * h, 32), sib, n2)
                n2 += 1
    for k in (3, 1):
        rearrange(0, (z + k) & 3, False)
        rearrange(1, (x + k) & 3, False)
    for j, k1 in enumerate(steps):
        for h in range(2):
            src = spot(h, k1, 2)
            for side in range(2):
                arrived(block(src, y, c, 32 * h + 16 * side, 16), v2, h * 8 + 2 * j + side)
            arrived(block(src, 1 - y, c, 32 * h, 32), far, h * 4 + j)
            both = pair(src, c, 32 * h, 32)
            send(both, both, sib, n, other_c)
            n += 1
    for k1 in steps:
        for h in range(2):
            arrived(pair(spot(h, k1, 2), oc, 32 * h, 32), sib, n2)
            n2 += 1

    @pl.when(row == 0)
    def _():
        head[0].wait_recv()

    @pl.when(pb < 63)
    def _():
        first.wait_recv()
    mine.wait()

    rearrange(0, (z + 2) & 3, False)
    rearrange(1, (x + 2) & 3, False)

    for t in range(4):
        for h in range(2):
            rearrange(h, t, True)

    def dots(t):
        w = rb[pl.ds(GROUP * t, GROUP)].reshape(GROUP * 128, E)
        v = lax.dot_general(qx[...], w, (((1,), (1,)), ((), ())), preferred_element_type=F32)
        for u in range(GROUP):
            s[GROUP * t + u, pl.ds(0, all_rows), :] = v[:, u * 128:(u + 1) * 128]
    for t in range(PLANES // GROUP):
        dots(t)

    ps = [steps_ref[0, d] for d in range(NDIR)]
    ss = [steps_ref[1, d] for d in range(NDIR)]
    three = [jnp.maximum(ps[d], ss[d]) == 3 for d in range(NDIR)]
    ns = [jnp.where(three[d], lengths[d] // 3, lengths[d] // 2) for d in range(NDIR)]
    phase = [lengths[d] - ns[d] * jnp.where(three[d], 3, 2) for d in range(NDIR)]
    weight = [1.0 / (lengths[d].astype(F32)) * (1.0 / math.sqrt(E)) for d in range(NDIR)]

    def tap(v, other, times):
        return jnp.where(v > other, times, jnp.where(times * v >= other, 1, 0))
    q1 = [tap(ps[d], ss[d], 1) for d in range(NDIR)]
    r1 = [tap(ss[d], ps[d], 1) for d in range(NDIR)]
    q2 = [tap(ps[d], ss[d], 2) for d in range(NDIR)]
    r2 = [tap(ss[d], ps[d], 2) for d in range(NDIR)]

    def step(d, b, r, s0):
        dp = ds[d][(b + ss[d]) & 3, pl.ds(r + ps[d], SUPER), :]
        t2 = s[jnp.where(three[d], b + r2[d], ZERO), pl.ds(r + q2[d], SUPER), :]
        t1 = s[b + r1[d], pl.ds(r + q1[d], SUPER), :]
        x2 = dp + t2
        x1 = x2 + t1
        x0 = x1 + s0
        e = jnp.where(phase[d] == 0, x0, jnp.where(phase[d] == 1, x1, x2))
        ds[d][b & 3, pl.ds(r, SUPER), :] = x0
        es[d][b & 31, pl.ds(r, SUPER), :] = e
        return x0

    def past(k, _):
        for b in (PLANES - 1 - 2 * k, PLANES - 2 - 2 * k):
            for r in range(0, all_rows, SUPER):
                s0 = s[b, pl.ds(r, SUPER), :]
                for d in range(NDIR):
                    step(d, b, r, s0)
        return 0
    lax.fori_loop(0, HALO // 2, past, 0)

    def inside(k, _):
        for b in (B - 1 - 2 * k, B - 2 - 2 * k):
            within(b)
        return 0

    def within(b):
        for r in range(0, all_rows, SUPER):
            s0 = s[b, pl.ds(r, SUPER), :]
            best = None
            for d in range(NDIR):
                x0 = step(d, b, r, s0)
                if r < rows:
                    en = es[d][(b + ns[d] * ss[d]) & 31, pl.ds(r + ns[d] * ps[d], SUPER), :]
                    v = (x0 - en) * weight[d]
                    best = v if best is None else jnp.maximum(best, v)
            if r < rows:
                o[b, pl.ds(r, SUPER), :] = best.astype(BF)
    outs = []
    for k in range(4):
        lax.fori_loop(4 * k, 4 * k + 4, inside, 0)
        part = pl.ds(B - 8 * k - 8, 8)
        copy = pltpu.make_async_copy(o.at[part], o_ref.at[part], osem.at[k])
        copy.start()
        outs.append(copy)
    for copy in sends:
        copy.wait_send()

    @pl.when(pb > 0)
    def _():
        first.wait_send()

    @pl.when((row == 1) & (z == 0) & (c == 0))
    def _():
        for copy in head:
            copy.wait_send()
    for copy in outs:
        copy.wait()


def untangle(o_ref, out_ref, o, perm, flat, isem, osem):
    rows = o_ref.shape[1]
    parts = 2
    size = rows // parts
    ins = [pltpu.make_async_copy(o_ref.at[:, pl.ds(k * size, size)], o.at[:, pl.ds(k * size, size)], isem.at[k]) for k in range(parts)]
    for copy in ins:
        copy.start()
    la = iota((128, 128), 0)
    ll = iota((128, 128), 1)

    def block_of(lane):
        n = lane & 63
        return jnp.where(lane < 64, n, ((n >> 2) & 3) * 16 + (n >> 4) * 4 + (n & 3))
    same = (block_of(la) & 1) * 2 + (la >> 6) == (ll >> 5)

    def make(q, _):
        perm[q] = jnp.where(same & (((block_of(la) >> 1) ^ (ll & 31)) == q), 1.0, 0.0).astype(BF)
        return 0
    lax.fori_loop(0, B, make, 0)
    lane = iota((16, 128), 1)
    bit = [[((v >> t) & 1).astype(F32).astype(BF) for t in range(5)] for v in (block_of(lane) >> 1, lane)]

    def network(v, way):
        for t in range(5):
            mask = bit[way][t] > 0.5
            v = [jnp.where(mask, v[q ^ (1 << t)], v[q]) for q in range(B)]
        return v
    outs = []
    for k in range(parts):
        ins[k].wait()

        def skew(i, _):
            r = pl.ds(pl.multiple_of(k * size + i * 16, 16), 16)
            v = network([o[q, r, :] for q in range(B)], 0)
            for q in range(B):
                o[q, r, :] = v[q]
            return 0
        lax.fori_loop(0, size // 16, skew, 0)

        def lanes(t, _):
            r = pl.ds(k * size, size)
            got = [jnp.dot(o[32 * t + u, r, :], perm[32 * t + u], preferred_element_type=F32).astype(BF) for u in range(32)]
            for u in range(32):
                o[32 * t + u, r, :] = got[u]
            return 0
        lax.fori_loop(0, B // 32, lanes, 0)

        def back(i, _):
            r = pl.ds(pl.multiple_of(k * size + i * 16, 16), 16)
            v = network([o[q, r, :] for q in range(B)], 1)
            for q in range(B):
                flat[r, q * 128:(q + 1) * 128] = v[q]
            return 0
        lax.fori_loop(0, size // 16, back, 0)
        part = pl.ds(k * size, size)
        copy = pltpu.make_async_copy(flat.at[part], out_ref.at[part], osem.at[k])
        copy.start()
        outs.append(copy)
    for copy in outs:
        copy.wait()


def per_device(queries, references, ratios, lengths):
    rows = queries.shape[0]
    cols = references.shape[1] * 64
    V, D, ANY = pltpu.VMEM, pltpu.SemaphoreType.DMA, pl.BlockSpec(memory_space=pl.ANY)
    all_rows = rows + TAIL
    o = pl.pallas_call(
        gather_and_smooth,
        out_shape=jax.ShapeDtypeStruct((B, rows, 128), BF),
        in_specs=[pl.BlockSpec(memory_space=pltpu.SMEM)] * 2 + [ANY] * 2,
        out_specs=ANY,
        scratch_shapes=[V((33, 128, E), BF), V((all_rows, E), BF), V((PLANES, 128, E), BF), V((ZERO + 1, all_rows + PAD, 128), F32)]
        + [V((4, all_rows + PAD, 128), F32)] * 4 + [V((32, all_rows + PAD, 128), F32)] * 4 + [V((B, rows, 128), BF)]
        + [D((2,)), D((2, 1)), D((2, 12)), D((2, 32)), D((2, 8)), D((2, 16)), D((2, 32)), D((2,)), D((9,)), D((4,))],
        compiler_params=pltpu.CompilerParams(collective_id=0, has_side_effects=True, vmem_limit_bytes=60 * 1024 * 1024),
        name="gather_and_smooth",
    )(ratios.T, lengths, queries, references)
    return pl.pallas_call(
        untangle,
        out_shape=jax.ShapeDtypeStruct((rows, cols), BF),
        in_specs=[ANY],
        out_specs=ANY,
        scratch_shapes=[V((B, rows, 128), BF), V((B, 128, 128), BF), V((rows, cols), BF), D((2,)), D((2,))],
        compiler_params=pltpu.CompilerParams(vmem_limit_bytes=60 * 1024 * 1024),
        name="untangle",
    )(o)


def solution(mesh):
    placed = (P("pb", None), P("row", "pb", None), P(), P())
    return jax.shard_map(
        per_device, mesh=mesh, in_specs=placed, out_specs=P("pb", "row"), check_vma=False
    )
```

```python
import math

import jax
import jax.numpy as jnp
from jax import lax
from jax.experimental import pallas as pl
from jax.experimental.pallas import tpu as pltpu
from jax.sharding import PartitionSpec as P

E = 512
NDIR = 4
B = 32
HALO = 24
PLANES = B + HALO
ZERO = 58
TAIL = 32
PAD = 8
SUPER = 32
GROUP = 56
MESH = pl.DeviceIdType.MESH
F32, BF = jnp.float32, jnp.bfloat16


def iota(shape, d):
    return lax.broadcasted_iota(jnp.int32, shape, d)


def gather_and_smooth(steps_ref, lengths, q_ref, r_ref, o_ref,
                      gv, qx, rb, s, d0, d1, d2, d3, e0, e1, e2, e3, o,
                      local, ysem, u1, v1, far, v2, sib, qsem, hsem, osem):
    rows = q_ref.shape[0]
    all_rows = rows + TAIL
    ds, es = (d0, d1, d2, d3), (e0, e1, e2, e3)
    pb, row = lax.axis_index("pb"), lax.axis_index("row")
    c, y, x, z = pb & 1, (pb >> 1) & 1, (pb >> 2) & 3, pb >> 4
    last = pb == 63
    me = (z, x)

    def at(zx, y_, c_):
        return ((zx[0] * 4 + zx[1]) * 2 + y_) * 2 + c_

    def place(h, k):
        return (z, (x + k) & 3) if h == 0 else ((z + k) & 3, x)

    def spot(h, k1, k2):
        return ((z + k2) & 3, (x + k1) & 3) if h == 0 else ((z + k1) & 3, (x + k2) & 3)

    other_y, other_c = at(me, 1 - y, c), at(me, y, 1 - c)

    bar = pltpu.get_barrier_semaphore()
    peers = [other_y, other_c] + [at(place(h, k), y_, c) for h in range(2) for k in (1, 2, 3) for y_ in (0, 1)]
    for dev in peers:
        pl.semaphore_signal(bar, inc=1, device_id={"pb": dev}, device_id_type=MESH)

    @pl.when(pb < 63)
    def _():
        pl.semaphore_signal(bar, inc=1, device_id={"pb": pb + 1}, device_id_type=MESH)

    @pl.when(row == 0)
    def _():
        pl.semaphore_signal(bar, inc=1, device_id={"pb": at((0, x), y, 0), "row": 1}, device_id_type=MESH)

    heads = jnp.where((row == 1) & (z == 0) & (c == 0), 8, 0)
    pl.semaphore_wait(bar, len(peers) + jnp.minimum(pb, 1) + heads)

    sends = []

    def send(src, dst, sems, k, dev):
        copy = pltpu.make_async_remote_copy(src_ref=src, dst_ref=dst, send_sem=sems.at[0, k], recv_sem=sems.at[1, k],
                                            device_id={"pb": dev}, device_id_type=MESH)
        copy.start()
        sends.append(copy)

    def arrived(dst, sems, k):
        pltpu.make_async_copy(dst, dst, sems.at[1, k]).wait()

    def block(zx, y_, c_, lo, size):
        return gv.at[(zx[0] * 4 + zx[1]) * 2 + y_, pl.ds(c_ * 64 + lo, size)]

    def pair(zx, c_, lo, size):
        return gv.at[pl.ds((zx[0] * 4 + zx[1]) * 2, 2), pl.ds(c_ * 64 + lo, size)]

    own = r_ref.at[0]
    keep = pltpu.make_async_copy(own, block(me, y, c, 0, 64), local.at[0])
    keep.start()
    send(own, block(me, y, c, 0, 64), ysem, 0, other_y)
    for k in (1, 3, 2):
        for h in range(2):
            for w in range(2):
                y_ = y if w == 0 else 1 - y
                send(r_ref.at[0, pl.ds(32 * h, 32)], block(me, y, c, 32 * h, 32), u1, h * 6 + (k - 1) * 2 + w, at(place(h, k), y_, c))
    send(own, block(me, y, c, 0, 64), sib, 0, other_c)
    first = pltpu.make_async_remote_copy(src_ref=q_ref.at[pl.ds(0, TAIL)], dst_ref=qx.at[pl.ds(rows, TAIL)], send_sem=qsem.at[0],
                                         recv_sem=qsem.at[1], device_id={"pb": jnp.maximum(pb - 1, 0)}, device_id_type=MESH)

    @pl.when(pb > 0)
    def _():
        first.start()

    mine = pltpu.make_async_copy(q_ref, qx.at[pl.ds(0, rows)], local.at[1])
    mine.start()

    none = jnp.zeros((TAIL, E), BF)

    @pl.when(last)
    def _():
        qx[pl.ds(rows, TAIL), :] = none

    @pl.when(row == 1)
    def _():
        gv[32, pl.ds(0, TAIL), :] = none

    zero = jnp.zeros((PAD, 128), F32)

    def clear(b, _):
        s[b, pl.ds(all_rows, PAD), :] = zero
        return 0
    lax.fori_loop(0, PLANES, clear, 0)
    for b in range(PLANES, ZERO + 1):
        s[b] = jnp.zeros((all_rows + PAD, 128), F32)
    for d in range(NDIR):
        for k in range(4):
            ds[d][k] = jnp.zeros((all_rows + PAD, 128), F32)

    ri = iota((256, 256), 0)
    ci = iota((256, 256), 1)
    turn = jnp.where(((ri >> 3) == (ci & 31)) & ((ri & 7) == (ci >> 5)), 1.0, 0.0).astype(BF)

    def rearrange(h, group, shifted):
        got = []
        for u in range(2):
            rows_of = []
            for i in range(4):
                hi, y_ = 2 * u + (i >> 1), i & 1
                k = (8 * group + 2 * hi if h == 0 else 8 * hi + 2 * group) + y_
                for core in range(2):
                    if not shifted:
                        part = gv[k, pl.ds(64 * core + 32 * h, 32), :]
                    elif h == 0:
                        part = gv[k, pl.ds(64 * core + 32, 32), :]
                    elif core == 0:
                        part = gv[k, pl.ds(64, 32), :]
                    else:
                        part = gv[k + 1, pl.ds(0, 32), :]
                    rows_of.append(part)
            planes = HALO if shifted else B
            got.append(jnp.dot(turn[:planes * 8], jnp.concatenate(rows_of, axis=0), preferred_element_type=F32).reshape(planes, 8, E))
        lanes = pl.ds(pl.multiple_of(64 * h + group * 16, 16), 16)
        rb[pl.ds(B if shifted else 0, got[0].shape[0]), lanes, :] = jnp.concatenate(got, axis=1).astype(BF)

    steps = (0, 3, 1, 2)

    def onward(h, j, w, src, dst):
        send(src, dst, v1, w * 16 + h * 8 + 2 * j, at(spot(h, 0, 1), y, c))
        send(src, dst, v1, w * 16 + h * 8 + 2 * j + 1, at(spot(h, 0, 3), y, c))
        if w:
            send(src, dst, far, h * 4 + j, at(spot(h, 0, 2), y, c))

    for h in range(2):
        onward(h, 0, 0, r_ref.at[0, pl.ds(32 * h, 32)], block(me, y, c, 32 * h, 32))
    for j, k1 in enumerate(steps):
        for h in range(2):
            if k1:
                p = block(place(h, k1), y, c, 32 * h, 32)
                arrived(p, u1, h * 6 + (3 - k1) * 2)
                onward(h, j, 0, p, p)
    n = 2
    for j, k1 in enumerate(steps):
        if not k1:
            arrived(block(me, 1 - y, c, 0, 64), ysem, 0)
        for h in range(2):
            p = block(place(h, k1), 1 - y, c, 32 * h, 32)
            if k1:
                arrived(p, u1, h * 6 + (3 - k1) * 2 + 1)
            onward(h, j, 1, p, p)
            if k1:
                both = pair(place(h, k1), c, 32 * h, 32)
                send(both, both, sib, n, other_c)
                n += 1
    theirs = block(me, 1 - y, c, 0, 64)
    send(theirs, theirs, sib, 1, other_c)

    keep.wait()
    head = [pltpu.make_async_remote_copy(src_ref=gv.at[0, pl.ds(0, TAIL)], dst_ref=gv.at[32, pl.ds(0, TAIL)], send_sem=hsem.at[k],
                                         recv_sem=hsem.at[8], device_id={"pb": at((k >> 1, x), y, k & 1), "row": 0}, device_id_type=MESH)
            for k in range(8)]

    @pl.when((row == 1) & (z == 0) & (c == 0))
    def _():
        for copy in head:
            copy.start()

    for j, k1 in enumerate(steps):
        for h in range(2):
            for side, k2 in ((0, 3), (1, 1)):
                src = spot(h, k1, k2)
                arrived(block(src, y, c, 32 * h, 32), v1, h * 8 + 2 * j + side)
                piece = block(src, y, c, 32 * h + 16 * side, 16)
                send(piece, piece, v2, h * 8 + 2 * j + side, at(spot(h, 0, 1 if side == 0 else 3), y, c))
    for j, k1 in enumerate(steps):
        for h in range(2):
            for side, k2 in ((0, 3), (1, 1)):
                src = spot(h, k1, k2)
                arrived(block(src, 1 - y, c, 32 * h, 32), v1, 16 + h * 8 + 2 * j + side)
                both = pair(src, c, 32 * h, 32)
                send(both, both, sib, n, other_c)
                n += 1
    oc = 1 - c
    arrived(block(me, y, oc, 0, 64), sib, 0)
    arrived(block(me, 1 - y, oc, 0, 64), sib, 1)
    n2 = 2
    for k1 in steps[1:]:
        for h in range(2):
            arrived(pair(place(h, k1), oc, 32 * h, 32), sib, n2)
            n2 += 1
    rearrange(0, z, False)
    rearrange(1, x, False)
    for k1 in steps:
        for h in range(2):
            for k2 in (3, 1):
                arrived(pair(spot(h, k1, k2), oc, 32 * h, 32), sib, n2)
                n2 += 1
    for j, k1 in enumerate(steps):
        for h in range(2):
            src = spot(h, k1, 2)
            for side in range(2):
                arrived(block(src, y, c, 32 * h + 16 * side, 16), v2, h * 8 + 2 * j + side)
            arrived(block(src, 1 - y, c, 32 * h, 32), far, h * 4 + j)
            both = pair(src, c, 32 * h, 32)
            send(both, both, sib, n, other_c)
            n += 1
    for k in (3, 1):
        rearrange(0, (z + k) & 3, False)
        rearrange(1, (x + k) & 3, False)
    for k1 in steps:
        for h in range(2):
            arrived(pair(spot(h, k1, 2), oc, 32 * h, 32), sib, n2)
            n2 += 1

    @pl.when(row == 0)
    def _():
        head[0].wait_recv()

    @pl.when(pb < 63)
    def _():
        first.wait_recv()
    mine.wait()

    rearrange(0, (z + 2) & 3, False)
    rearrange(1, (x + 2) & 3, False)

    for t in range(4):
        for h in range(2):
            rearrange(h, t, True)

    def dots(t):
        w = rb[pl.ds(GROUP * t, GROUP)].reshape(GROUP * 128, E)
        v = lax.dot_general(qx[...], w, (((1,), (1,)), ((), ())), preferred_element_type=F32)
        for u in range(GROUP):
            s[GROUP * t + u, pl.ds(0, all_rows), :] = v[:, u * 128:(u + 1) * 128]
    for t in range(PLANES // GROUP):
        dots(t)

    ps = [steps_ref[0, d] for d in range(NDIR)]
    ss = [steps_ref[1, d] for d in range(NDIR)]
    three = [jnp.maximum(ps[d], ss[d]) == 3 for d in range(NDIR)]
    ns = [jnp.where(three[d], lengths[d] // 3, lengths[d] // 2) for d in range(NDIR)]
    phase = [lengths[d] - ns[d] * jnp.where(three[d], 3, 2) for d in range(NDIR)]
    weight = [1.0 / (lengths[d].astype(F32)) * (1.0 / math.sqrt(E)) for d in range(NDIR)]

    def tap(v, other, times):
        return jnp.where(v > other, times, jnp.where(times * v >= other, 1, 0))
    q1 = [tap(ps[d], ss[d], 1) for d in range(NDIR)]
    r1 = [tap(ss[d], ps[d], 1) for d in range(NDIR)]
    q2 = [tap(ps[d], ss[d], 2) for d in range(NDIR)]
    r2 = [tap(ss[d], ps[d], 2) for d in range(NDIR)]

    def step(d, b, r, s0):
        dp = ds[d][(b + ss[d]) & 3, pl.ds(r + ps[d], SUPER), :]
        t2 = s[jnp.where(three[d], b + r2[d], ZERO), pl.ds(r + q2[d], SUPER), :]
        t1 = s[b + r1[d], pl.ds(r + q1[d], SUPER), :]
        x2 = dp + t2
        x1 = x2 + t1
        x0 = x1 + s0
        e = jnp.where(phase[d] == 0, x0, jnp.where(phase[d] == 1, x1, x2))
        ds[d][b & 3, pl.ds(r, SUPER), :] = x0
        es[d][b & 31, pl.ds(r, SUPER), :] = e
        return x0

    def past(k, _):
        for b in [PLANES - 1 - u - 4 * k for u in range(4)]:
            for r in range(0, all_rows, SUPER):
                s0 = s[b, pl.ds(r, SUPER), :]
                for d in range(NDIR):
                    step(d, b, r, s0)
        return 0
    lax.fori_loop(0, HALO // 4, past, 0)

    def inside(k, _):
        for b in [B - 1 - u - 4 * k for u in range(4)]:
            within(b)
        return 0

    def within(b):
        for r in range(0, all_rows, SUPER):
            s0 = s[b, pl.ds(r, SUPER), :]
            best = None
            for d in range(NDIR):
                x0 = step(d, b, r, s0)
                if r < rows:
                    en = es[d][(b + ns[d] * ss[d]) & 31, pl.ds(r + ns[d] * ps[d], SUPER), :]
                    v = (x0 - en) * weight[d]
                    best = v if best is None else jnp.maximum(best, v)
            if r < rows:
                o[b, pl.ds(r, SUPER), :] = best.astype(BF)
    outs = []
    for k in range(4):
        lax.fori_loop(2 * k, 2 * k + 2, inside, 0)
        part = pl.ds(B - 8 * k - 8, 8)
        copy = pltpu.make_async_copy(o.at[part], o_ref.at[part], osem.at[k])
        copy.start()
        outs.append(copy)
    for copy in sends:
        copy.wait_send()

    @pl.when(pb > 0)
    def _():
        first.wait_send()

    @pl.when((row == 1) & (z == 0) & (c == 0))
    def _():
        for copy in head:
            copy.wait_send()
    for copy in outs:
        copy.wait()


def untangle(o_ref, out_ref, o, perm, flat, isem, osem):
    rows = o_ref.shape[1]
    parts = 2
    size = rows // parts
    ins = [pltpu.make_async_copy(o_ref.at[:, pl.ds(k * size, size)], o.at[:, pl.ds(k * size, size)], isem.at[k]) for k in range(parts)]
    for copy in ins:
        copy.start()
    la = iota((128, 128), 0)
    ll = iota((128, 128), 1)

    def block_of(lane):
        n = lane & 63
        return jnp.where(lane < 64, n, ((n >> 2) & 3) * 16 + (n >> 4) * 4 + (n & 3))
    same = (block_of(la) & 1) * 2 + (la >> 6) == (ll >> 5)

    def make(q, _):
        perm[q] = jnp.where(same & (((block_of(la) >> 1) ^ (ll & 31)) == q), 1.0, 0.0).astype(BF)
        return 0
    lax.fori_loop(0, B, make, 0)
    lane = iota((16, 128), 1)
    bit = [[((v >> t) & 1).astype(F32).astype(BF) for t in range(5)] for v in (block_of(lane) >> 1, lane)]

    def network(v, way):
        for t in range(5):
            mask = bit[way][t] > 0.5
            v = [jnp.where(mask, v[q ^ (1 << t)], v[q]) for q in range(B)]
        return v
    outs = []
    for k in range(parts):
        ins[k].wait()

        def skew(i, _):
            r = pl.ds(pl.multiple_of(k * size + i * 16, 16), 16)
            v = network([o[q, r, :] for q in range(B)], 0)
            for q in range(B):
                o[q, r, :] = v[q]
            return 0
        lax.fori_loop(0, size // 16, skew, 0)

        def lanes(t, _):
            r = pl.ds(k * size, size)
            got = [jnp.dot(o[32 * t + u, r, :], perm[32 * t + u], preferred_element_type=F32).astype(BF) for u in range(32)]
            for u in range(32):
                o[32 * t + u, r, :] = got[u]
            return 0
        lax.fori_loop(0, B // 32, lanes, 0)

        def back(i, _):
            r = pl.ds(pl.multiple_of(k * size + i * 16, 16), 16)
            v = network([o[q, r, :] for q in range(B)], 1)
            for q in range(B):
                flat[r, q * 128:(q + 1) * 128] = v[q]
            return 0
        lax.fori_loop(0, size // 16, back, 0)
        part = pl.ds(k * size, size)
        copy = pltpu.make_async_copy(flat.at[part], out_ref.at[part], osem.at[k])
        copy.start()
        outs.append(copy)
    for copy in outs:
        copy.wait()


def per_device(queries, references, ratios, lengths):
    rows = queries.shape[0]
    cols = references.shape[1] * 64
    V, D, ANY = pltpu.VMEM, pltpu.SemaphoreType.DMA, pl.BlockSpec(memory_space=pl.ANY)
    all_rows = rows + TAIL
    o = pl.pallas_call(
        gather_and_smooth,
        out_shape=jax.ShapeDtypeStruct((B, rows, 128), BF),
        in_specs=[pl.BlockSpec(memory_space=pltpu.SMEM)] * 2 + [ANY] * 2,
        out_specs=ANY,
        scratch_shapes=[V((33, 128, E), BF), V((all_rows, E), BF), V((PLANES, 128, E), BF), V((ZERO + 1, all_rows + PAD, 128), F32)]
        + [V((4, all_rows + PAD, 128), F32)] * 4 + [V((32, all_rows + PAD, 128), F32)] * 4 + [V((B, rows, 128), BF)]
        + [D((2,)), D((2, 1)), D((2, 12)), D((2, 32)), D((2, 8)), D((2, 16)), D((2, 32)), D((2,)), D((9,)), D((4,))],
        compiler_params=pltpu.CompilerParams(collective_id=0, has_side_effects=True, vmem_limit_bytes=60 * 1024 * 1024),
        name="gather_and_smooth",
    )(ratios.T, lengths, queries, references)
    return pl.pallas_call(
        untangle,
        out_shape=jax.ShapeDtypeStruct((rows, cols), BF),
        in_specs=[ANY],
        out_specs=ANY,
        scratch_shapes=[V((B, rows, 128), BF), V((B, 128, 128), BF), V((rows, cols), BF), D((2,)), D((2,))],
        compiler_params=pltpu.CompilerParams(vmem_limit_bytes=60 * 1024 * 1024),
        name="untangle",
    )(o)


def solution(mesh):
    placed = (P("pb", None), P("row", "pb", None), P(), P())
    return jax.shard_map(
        per_device, mesh=mesh, in_specs=placed, out_specs=P("pb", "row"), check_vma=False
    )
```
